1024 devices in a mesh: dp: 64 (over y, z), expert: 16 (over x, core).
Axes of the slice: x: 8, y: 8, z: 8, core: 2. Of those that a mesh axis runs over, the one named last changes fastest.
Arguments:
- tokens: bfloat16 [16, 128, 7168], P('expert', 'dp'), may hold values from -6 to 6
- slot_grads: bfloat16 [16, 128, 8, 2048], P('expert', 'dp'), may hold values from -0.796875 to 0.796875
- expert_ids: int32 [16, 128, 8], P('expert'), may hold values from 0 to 31, all different within a row; in each aligned block of 128 rows (0 to 127, 128 to 255, ..., all dimensions but the last counted through in order) at most 48 rows name the same one
Outputs:
- weight_grad: bfloat16 [32, 64, 896, 256], P('expert', 'dp')
The draws below stay inside these ranges and needn't reach their ends.
Inputs may be any that keep to these rules, and one draw needn't show every extreme that they name: `expert_ids`: each token names 8 different experts. Among the 128 tokens of one group, no expert is named by more than 48 tokens, a bound that some block reaches.
All inputs are finite; a program needn't handle non-finite values.
Results may differ from the reference program's by a relative error of at most 0.001.
Values may be sent and summed in bfloat16 or wider, within the bound.
No kernel may reach another device: no remote copies, remote signals or barrier semaphores. Data moves between devices by JAX's collectives and lax.ppermute only.
A program may use at most 128 MiB of HBM per device.

```python
import math
import jax
import jax.numpy as jnp
import numpy as np
from jax import lax

D = 7168
FF = 2048
TOP = 8
DB = 8
FB = 8
DBLK = 896
FBLK = 256
GROUPS = 16
TOK_EX = 128
EXPERTS = 32
CAP = 48
N_DP = 64


def steps_of(own_key, dims, split, low, high):
    def one(axis_at, blocks):
        heights = jax.random.uniform(jax.random.fold_in(jax.random.fold_in(own_key, 6), axis_at), (blocks,), jnp.float32, low / len(split), high / len(split))
        return jnp.repeat(jnp.exp(heights), dims[axis_at] // blocks).reshape((-1,) + (1,) * (len(dims) - axis_at - 1))

    loudness = one(*split[0])
    for cut in split[1:]:
        loudness = loudness * one(*cut)
    return loudness


def shared_out(stream_key, own, number, rows, number_of, top, bound, lean):
    ranking = jax.random.permutation(stream_key, number_of)
    packed, ordinary = shares(number_of, rows * top, bound, lean, True), shares(number_of, rows * top, bound, lean, False)
    places = jnp.arange(number_of)

    def named(tallies, rotation):
        used = int((tallies > 0).sum())
        fixed = max(1, used // 4)
        passed = fixed + (places - fixed + rotation * (used - fixed)) % max(1, number_of - fixed)
        return jnp.zeros((number_of,), jnp.int32).at[ranking[jnp.where(places < fixed, places, passed)]].set(jnp.asarray(tallies, jnp.int32))

    tallies = jnp.where(number % 4 == 0, named(packed, number // 4), named(ordinary, number - number // 4 - 1))
    mixed = jax.random.permutation(jax.random.fold_in(own, 3), number_of)
    giver, sink = mixed[0:number_of // 2 * 2:2], mixed[1:number_of // 2 * 2:2]
    slack = jnp.minimum(tallies[giver] - 1, bound - tallies[sink]) // 2
    slack = jnp.where((giver == ranking[0]) | (sink == ranking[0]) | (tallies[sink] == 0), 0, jnp.maximum(slack, 0))
    passed = jax.random.randint(jax.random.fold_in(own, 4), (number_of // 2,), 0, 1 << 20) % (slack + 1)
    tallies = tallies.at[giver].add(-passed).at[sink].add(passed)
    items = jnp.searchsorted(jnp.cumsum(tallies), jnp.arange(rows * top), side="right").astype(jnp.int32)
    table = items.reshape(top, rows).T
    table = table[jax.random.permutation(jax.random.fold_in(own, 1), rows)]
    rotation = jax.random.randint(jax.random.fold_in(own, 2), (rows, 1), 0, top)
    return jnp.take_along_axis(table, (jnp.arange(top)[None, :] + rotation) % top, axis=1)


def shares(number_of, total, reach, lean, full):
    portions = [(1 << 20) // math.isqrt(rank ** lean) + 1 for rank in range(1, number_of + 1)]
    largest = reach if full else min(reach, max(-(-total // number_of), total * portions[0] // sum(portions)))
    least = 1 if total - largest >= number_of - 1 else 0
    counts, spare = [largest] + [least] * (number_of - 1), total - largest - least * (number_of - 1)
    while spare > 0:
        candidates = [i for i in range(1, number_of) if counts[i] < largest] or [i for i in range(1, number_of) if counts[i] < reach]
        mass, budget = sum([portions[i] for i in candidates]), spare
        for i in candidates:
            more = min(reach - counts[i], max(1, budget * portions[i] // mass), spare)
            counts[i] = counts[i] + more
            spare = spare - more
    return np.array(counts)


def noise(stream_key, extent, width, limit, cuts=(), held_as=jnp.bfloat16):
    entries = jax.random.normal(stream_key, extent, jnp.float32) * width
    if len(cuts) > 0:
        entries = steps_of(stream_key, extent, cuts, -0.22, 0.18) * entries
    return jnp.clip(entries, min=-limit, max=limit).astype(held_as)


def setup_inputs(seed: int = 0) -> dict:
    keys = jax.random.split(jax.random.key(seed), 4)
    tokens = noise(keys[0], (GROUPS, TOK_EX, D), 1.0, 6.0, ((0, 16), (1, 64)))
    slot_grads = noise(keys[1], (GROUPS, TOK_EX, TOP, FF), 0.1, 0.796875, ((0, 16), (1, 64)))
    expert_ids_keys = jax.random.split(jax.random.fold_in(keys[2], 1), GROUPS * TOK_EX // TOK_EX)
    expert_ids_turns = jax.random.permutation(jax.random.fold_in(keys[2], 3), GROUPS * TOK_EX // TOK_EX)
    expert_ids = jax.vmap(lambda own, number: shared_out(jax.random.fold_in(keys[2], 2), own, number, TOK_EX, EXPERTS, TOP, CAP, 2))(expert_ids_keys, expert_ids_turns).reshape((GROUPS, TOK_EX, TOP))
    return dict(tokens=tokens, slot_grads=slot_grads, expert_ids=expert_ids)


def slot_buffers(group_tokens, group_grads, group_ids):
    flat_ids = group_ids.reshape(-1).astype(jnp.int32)
    hits = (flat_ids[:, None] == jnp.arange(EXPERTS, dtype=jnp.int32)[None, :]).astype(jnp.int32)
    ranks = jnp.sum((jnp.cumsum(hits, axis=0) - hits) * hits, axis=1).astype(jnp.int32)
    target = flat_ids * CAP + ranks
    source = jnp.zeros((EXPERTS * CAP,), jnp.int32).at[target].set(jnp.arange(flat_ids.shape[0], dtype=jnp.int32) + 1)
    filled = source > 0
    slot_index = jnp.maximum(source - 1, 0).astype(jnp.int32)
    rows_x = jnp.where(filled[:, None], group_tokens[slot_index // TOP], jnp.zeros((), group_tokens.dtype))
    rows_g = jnp.where(filled[:, None], group_grads.reshape(-1, FF)[slot_index], jnp.zeros((), group_grads.dtype))
    return rows_x.reshape(EXPERTS, CAP, D), rows_g.reshape(EXPERTS, CAP, FF)


def reference(tokens, slot_grads, expert_ids):
    left_all, right_all = jax.vmap(slot_buffers)(tokens, slot_grads, expert_ids)

    def one_expert(expert):
        left = lax.dynamic_index_in_dim(left_all, expert, 1, keepdims=False).reshape(-1, D)
        right = lax.dynamic_index_in_dim(right_all, expert, 1, keepdims=False).reshape(-1, FF)
        full = jnp.dot(left.T, right, preferred_element_type=jnp.float32)
        blocks = full.reshape(DB, DBLK, FB, FBLK).transpose(0, 2, 1, 3).reshape(N_DP, DBLK, FBLK)
        return blocks.astype(jnp.bfloat16)

    return lax.map(one_expert, jnp.arange(EXPERTS, dtype=jnp.int32))
```

```python
import functools

import jax
import jax.numpy as jnp
from jax import lax
from jax.experimental import pallas as pl
from jax.experimental.pallas import tpu as pltpu
from jax.sharding import Mesh, PartitionSpec as P

DB = 8
FB = 8
TOP = 8
TOK = 128
DBLK = 896
FBLK = 256
PIECE = FBLK // DB
EXPERTS = 32
CAP = 48
OWN = 2
OWNERS = 16
HALF = CAP // 2
LANES = 128
XROWS = DBLK + 16
STEP_ROWS = 224


def earlier():
    row = lax.broadcasted_iota(jnp.int32, (TOK, TOK), 0)
    col = lax.broadcasted_iota(jnp.int32, (TOK, TOK), 1)
    return (row < col).astype(jnp.bfloat16)


def place_kernel(ids_ref, onehot_ref):
    expert = lax.broadcasted_iota(jnp.int32, (EXPERTS, TOK), 0)
    named = jnp.zeros((EXPERTS, TOK), jnp.float32)
    for k in range(TOP):
        named += (ids_ref[k : k + 1, :] == expert).astype(jnp.float32)
    before = jnp.dot(named.astype(jnp.bfloat16), earlier(), preferred_element_type=jnp.float32)
    place = before.astype(jnp.int32) + CAP * expert
    row = lax.broadcasted_iota(jnp.int32, (OWNERS * HALF, TOK), 0)
    owner = row // HALF
    base = owner * (OWN * CAP) + (row - owner * HALF)
    for k in range(TOP):
        target = jnp.sum(
            jnp.where(ids_ref[k : k + 1, :] == expert, place, 0), axis=0, keepdims=True
        )
        for j in range(4):
            at = (j * TOP + k) * TOK
            onehot_ref[:, at : at + TOK] = (base + j * HALF == target).astype(jnp.bfloat16)


def route_kernel(pieces_ref, onehot_ref, out_ref):
    pieces = pieces_ref[...].astype(jnp.float32)
    block = lax.broadcasted_iota(jnp.int32, (TOK, LANES), 1) // PIECE
    rows = []
    for j in range(4):
        for k in range(TOP):
            half = pieces[:, (k // 4) * LANES : (k // 4 + 1) * LANES]
            shift = ((j - k) % 4) * PIECE
            moved = pltpu.roll(half, shift, 1) if shift else half
            rows.append(jnp.where(block == j, moved, 0.0).astype(jnp.bfloat16))
    out_ref[...] = jnp.dot(
        onehot_ref[...], jnp.concatenate(rows, axis=0), preferred_element_type=jnp.float32
    ).astype(jnp.bfloat16)


def spread_kernel(slots_ref, out_ref):
    source = lax.broadcasted_iota(jnp.int32, (DB * LANES, FBLK), 0)
    column = lax.broadcasted_iota(jnp.int32, (DB * LANES, FBLK), 1)
    slots = jnp.concatenate([slots_ref[y] for y in range(DB)], axis=1)
    wanted = (column // PIECE) * LANES + column % PIECE
    for j in range(4):
        pick = (source == wanted + j * PIECE).astype(jnp.bfloat16)
        out_ref[j] = jnp.dot(slots, pick, preferred_element_type=jnp.float32).astype(jnp.bfloat16)


def product_kernel(first_ref, x_ref, ids_ref, slots_ref, out_ref, dense_ref):
    @pl.when(pl.program_id(0) == 0)
    def _():
        named = []
        for e in range(OWN):
            for g in range(OWNERS):
                hit = (ids_ref[g, 0:TOP, :].astype(jnp.int32) == first_ref[0] + e).astype(jnp.float32)
                named.append(jnp.sum(hit, axis=0, keepdims=True))
        named = jnp.concatenate(named, axis=0)
        before = jnp.dot(named.astype(jnp.bfloat16), earlier(), preferred_element_type=jnp.float32)
        place = jnp.where(named > 0.0, before, -1.0).T
        number = lax.broadcasted_iota(jnp.int32, (TOK, CAP), 1).astype(jnp.float32)
        for e in range(OWN):
            for g in range(OWNERS):
                at = e * OWNERS + g
                pick = (place[:, at : at + 1] == number).astype(jnp.bfloat16)
                dense_ref[g * TOK : (g + 1) * TOK, e * FBLK : (e + 1) * FBLK] = jnp.dot(
                    pick, slots_ref[e, g], preferred_element_type=jnp.float32
                ).astype(jnp.bfloat16)

    left = jnp.concatenate([x_ref[g] for g in range(OWNERS)], axis=1)
    total = jnp.dot(left, dense_ref[...], preferred_element_type=jnp.float32)
    for e in range(OWN):
        out_ref[e] = total[:, e * FBLK : (e + 1) * FBLK].astype(jnp.bfloat16)


def params(mib):
    return pltpu.CompilerParams(vmem_limit_bytes=mib << 20)


def body(tokens, slot_grads, expert_ids):
    ids = expert_ids[0].T
    onehot = pl.pallas_call(
        place_kernel,
        out_shape=jax.ShapeDtypeStruct((OWNERS * HALF, 4 * TOP * TOK), jnp.bfloat16),
        compiler_params=params(16),
    )(ids)

    x_part = tokens[0].reshape(2, DB, DBLK).transpose(1, 0, 2)
    x_part = jnp.broadcast_to(x_part[:, None], (DB, FB, 2, DBLK))
    g_part = slot_grads[0].reshape(2, TOP, FB, DB, PIECE).transpose(3, 2, 0, 1, 4)
    g_part = g_part.reshape(DB, FB, 2, TOP * PIECE)
    send = jnp.concatenate([x_part, g_part], axis=3).reshape(DB * FB, 2, DBLK + FBLK)
    got = lax.all_to_all(send, ("y", "z"), split_axis=0, concat_axis=0, tiled=True)
    got = got.reshape(TOK, DBLK + FBLK)

    id_rows = jnp.concatenate([ids, jnp.zeros((8, TOK), jnp.int32)], axis=0)
    left = jnp.concatenate([got[:, :DBLK].T, id_rows.astype(jnp.bfloat16)], axis=0)
    left = lax.all_gather(left, ("x", "core"))

    routed = pl.pallas_call(
        route_kernel,
        out_shape=jax.ShapeDtypeStruct((OWNERS * HALF, LANES), jnp.bfloat16),
        compiler_params=params(32),
    )(got[:, DBLK:], onehot)
    routed = lax.all_to_all(
        routed.reshape(OWNERS, HALF, LANES), ("x", "core"), split_axis=0, concat_axis=0, tiled=True
    )
    slots = lax.all_to_all(
        jnp.broadcast_to(routed[None], (DB, OWNERS, HALF, LANES)),
        "y",
        split_axis=0,
        concat_axis=0,
        tiled=True,
    )
    spread = pl.pallas_call(
        spread_kernel,
        out_shape=jax.ShapeDtypeStruct((4, OWNERS * HALF, FBLK), jnp.bfloat16),
        compiler_params=params(32),
    )(slots.reshape(DB, OWNERS * HALF, LANES))
    spread = spread.reshape(OWN, 2, OWNERS, HALF, FBLK).transpose(0, 2, 1, 3, 4)
    spread = spread.reshape(OWN, OWNERS, CAP, FBLK)

    first = (OWN * lax.axis_index(("x", "core"))).astype(jnp.int32).reshape(1)
    out = pl.pallas_call(
        product_kernel,
        grid=(DBLK // STEP_ROWS,),
        in_specs=[
            pl.BlockSpec(memory_space=pltpu.SMEM),
            pl.BlockSpec((OWNERS, STEP_ROWS, TOK), lambda i: (0, i, 0)),
            pl.BlockSpec((OWNERS, 16, TOK), lambda i: (0, DBLK // 16, 0)),
            pl.BlockSpec((OWN, OWNERS, CAP, FBLK), lambda i: (0, 0, 0, 0)),
        ],
        out_specs=pl.BlockSpec((OWN, STEP_ROWS, FBLK), lambda i: (0, i, 0)),
        out_shape=jax.ShapeDtypeStruct((OWN, DBLK, FBLK), jnp.bfloat16),
        scratch_shapes=[pltpu.VMEM((OWNERS * TOK, OWN * FBLK), jnp.bfloat16)],
        compiler_params=params(32),
    )(first, left, left, spread)
    return out[:, None]


def solution(mesh):
    grid = Mesh(mesh.devices.reshape(DB, FB, 8, 2), ("y", "z", "x", "core"))
    owner, block = ("x", "core"), ("y", "z")
    placed = (P(owner, block, None), P(owner, block, None, None), P(owner, None, None))
    return jax.shard_map(
        body, mesh=grid, in_specs=placed, out_specs=P(owner, block, None, None), check_vma=False
    )
```

```python
import jax
import jax.numpy as jnp
from jax import lax
from jax.experimental import pallas as pl
from jax.experimental.pallas import tpu as pltpu
from jax.sharding import Mesh, PartitionSpec as P

DB = 8
FB = 8
TOP = 8
TOK = 128
DBLK = 896
FBLK = 256
PIECE = FBLK // DB
EXPERTS = 32
CAP = 48
OWN = 2
OWNERS = 16
HALF = CAP // 2
LANES = 128
SWAP = DBLK // 2
PART = 128


def earlier():
    row = lax.broadcasted_iota(jnp.int32, (TOK, TOK), 0)
    col = lax.broadcasted_iota(jnp.int32, (TOK, TOK), 1)
    return (row < col).astype(jnp.bfloat16)


def place_kernel(ids_ref, onehot_ref):
    expert = lax.broadcasted_iota(jnp.int32, (EXPERTS, TOK), 0)
    named = jnp.zeros((EXPERTS, TOK), jnp.float32)
    for k in range(TOP):
        named += (ids_ref[k : k + 1, :] == expert).astype(jnp.float32)
    before = jnp.dot(named.astype(jnp.bfloat16), earlier(), preferred_element_type=jnp.float32)
    place = before.astype(jnp.int32) + CAP * expert
    row = lax.broadcasted_iota(jnp.int32, (OWNERS * HALF, TOK), 0)
    owner = row // HALF
    base = owner * (OWN * CAP) + (row - owner * HALF)
    for k in range(TOP):
        target = jnp.sum(
            jnp.where(ids_ref[k : k + 1, :] == expert, place, 0), axis=0, keepdims=True
        )
        for j in range(4):
            at = (j * TOP + k) * TOK
            onehot_ref[:, at : at + TOK] = (base + j * HALF == target).astype(jnp.bfloat16)


def pack_kernel(got_ref, onehot_ref, ids_ref, first_ref, left_ref):
    left = got_ref[:, :DBLK].T
    left_ref[...] = left
    pieces = got_ref[:, DBLK:].astype(jnp.float32)
    block = lax.broadcasted_iota(jnp.int32, (TOK, LANES), 1) // PIECE
    rows = []
    for j in range(4):
        for k in range(TOP):
            half = pieces[:, (k // 4) * LANES : (k // 4 + 1) * LANES]
            shift = ((j - k) % 4) * PIECE
            moved = pltpu.roll(half, shift, 1) if shift else half
            rows.append(jnp.where(block == j, moved, 0.0).astype(jnp.bfloat16))
    routed = jnp.dot(
        onehot_ref[...], jnp.concatenate(rows, axis=0), preferred_element_type=jnp.float32
    )
    ids = ids_ref[...].astype(jnp.float32)
    for d in range(OWNERS):
        at = (d % 2) * SWAP
        first_ref[d, :PART, :] = left[at : at + PART]
        first_ref[d, PART:, :] = jnp.concatenate(
            [routed[d * HALF : (d + 1) * HALF], ids], axis=0
        ).astype(jnp.bfloat16)


def dense_kernel(info_ref, ids_ref, *refs):
    dense_ref = refs[DB]
    slots = jnp.concatenate([refs[s][...] for s in range(DB)], axis=1)
    source = lax.broadcasted_iota(jnp.int32, (DB * LANES, FBLK), 0)
    column = lax.broadcasted_iota(jnp.int32, (DB * LANES, FBLK), 1)
    lane = source % LANES
    wanted = ((info_ref[1] + DB - source // LANES) % DB) * PIECE + lane % PIECE
    spread = []
    for j in range(4):
        pick = ((column == wanted) & (lane // PIECE == j)).astype(jnp.bfloat16)
        spread.append(jnp.dot(slots, pick, preferred_element_type=jnp.float32))
    named = []
    for e in range(OWN):
        for g in range(OWNERS):
            hit = (ids_ref[g].astype(jnp.int32) == info_ref[0] + e).astype(jnp.float32)
            named.append(jnp.sum(hit, axis=0, keepdims=True))
    named = jnp.concatenate(named, axis=0)
    before = jnp.dot(named.astype(jnp.bfloat16), earlier(), preferred_element_type=jnp.float32)
    place = jnp.where(named > 0.0, before, -1.0).T
    number = lax.broadcasted_iota(jnp.int32, (TOK, CAP), 1).astype(jnp.float32)
    for e in range(OWN):
        for g in range(OWNERS):
            at = e * OWNERS + g
            pick = (place[:, at : at + 1] == number).astype(jnp.bfloat16)
            rows = slice(g * HALF, (g + 1) * HALF)
            value = jnp.concatenate([spread[2 * e][rows], spread[2 * e + 1][rows]], axis=0)
            dense_ref[g * TOK : (g + 1) * TOK, e * FBLK : (e + 1) * FBLK] = jnp.dot(
                pick, value.astype(jnp.bfloat16), preferred_element_type=jnp.float32
            ).astype(jnp.bfloat16)


def product_kernel(side_ref, first_ref, rest_ref, dense_ref, *refs):
    del side_ref
    out_ref = refs[-1]
    left = [jnp.concatenate([first_ref[g], rest_ref[g]], axis=0) for g in range(OWNERS)]
    total = jnp.dot(
        jnp.concatenate(left, axis=1), dense_ref[...], preferred_element_type=jnp.float32
    )
    for e in range(OWN):
        out_ref[e] = total[:, e * FBLK : (e + 1) * FBLK].astype(jnp.bfloat16)


def params(mib):
    return pltpu.CompilerParams(vmem_limit_bytes=mib << 20)


def cost(flops, size):
    return pl.CostEstimate(flops=flops, bytes_accessed=size, transcendentals=0)


def product(side, first, rest, dense, out):
    specs = [
        pl.BlockSpec((OWNERS, PART, TOK), lambda i, s: (0, 0, 0)),
        pl.BlockSpec((OWNERS, SWAP - PART, TOK), lambda i, s: (0, 0, 0)),
        pl.BlockSpec((OWNERS * TOK, OWN * FBLK), lambda i, s: (0, 0)),
    ]
    args = [side, first, rest, dense]
    if out is not None:
        specs.append(pl.BlockSpec(memory_space=pl.ANY))
        args.append(out)
    return pl.pallas_call(
        product_kernel,
        grid_spec=pltpu.PrefetchScalarGridSpec(
            num_scalar_prefetch=1,
            grid=(1,),
            in_specs=specs,
            out_specs=pl.BlockSpec((OWN, SWAP, FBLK), lambda i, s: (0, s[0], 0)),
        ),
        out_shape=jax.ShapeDtypeStruct((OWN, DBLK, FBLK), jnp.bfloat16),
        input_output_aliases={} if out is None else {4: 0},
        cost_estimate=cost(2 * SWAP * 2048 * 512, 5 << 20),
        compiler_params=params(32),
    )(*args)


def body(tokens, slot_grads, expert_ids):
    ids = expert_ids[0].T
    onehot = pl.pallas_call(
        place_kernel,
        out_shape=jax.ShapeDtypeStruct((OWNERS * HALF, 4 * TOP * TOK), jnp.bfloat16),
        cost_estimate=cost(1 << 22, 6 << 20),
        compiler_params=params(16),
    )(ids)

    x_part = tokens[0].reshape(2, DB, DBLK).transpose(1, 0, 2)
    x_part = jnp.broadcast_to(x_part[:, None], (DB, FB, 2, DBLK))
    g_part = slot_grads[0].reshape(2, TOP, FB, DB, PIECE).transpose(3, 2, 0, 1, 4)
    g_part = g_part.reshape(DB, FB, 2, TOP * PIECE)
    send = jnp.concatenate([x_part, g_part], axis=3).reshape(DB * FB, 2, DBLK + FBLK)
    got = lax.all_to_all(send, ("y", "z"), split_axis=0, concat_axis=0, tiled=True)
    got = got.reshape(TOK, DBLK + FBLK)

    first, left = pl.pallas_call(
        pack_kernel,
        out_shape=(
            jax.ShapeDtypeStruct((OWNERS, PART + 32, TOK), jnp.bfloat16),
            jax.ShapeDtypeStruct((DBLK, TOK), jnp.bfloat16),
        ),
        cost_estimate=cost(1 << 29, 6 << 20),
        compiler_params=params(32),
    )(got, onehot, ids)
    owner = ("x", "core")
    first = lax.all_to_all(first, owner, split_axis=0, concat_axis=0, tiled=True)
    rest = left.reshape(2, SWAP, TOK)[:, PART:]
    rest = jnp.broadcast_to(rest[None], (8, 2, SWAP - PART, TOK)).reshape(OWNERS, SWAP - PART, TOK)
    group_ids = first[:, PART + HALF :]
    rest, group_ids = lax.optimization_barrier((rest, group_ids))
    rest = lax.all_to_all(rest, owner, split_axis=0, concat_axis=0, tiled=True)

    routed = first[:, PART : PART + HALF].reshape(OWNERS * HALF, LANES)
    slots = [routed] + [
        lax.ppermute(routed, "y", [(i, (i + s) % DB) for i in range(DB)]) for s in range(1, DB)
    ]
    across = [(0, 1), (1, 0)]
    own = first[:, :PART]
    first_across = lax.ppermute(own, "core", across)
    core = lax.axis_index("core")
    info = jnp.stack([OWN * lax.axis_index(owner), lax.axis_index("y")]).astype(jnp.int32)
    dense = pl.pallas_call(
        dense_kernel,
        in_specs=[pl.BlockSpec(memory_space=pltpu.SMEM)]
        + [pl.BlockSpec(memory_space=pltpu.VMEM)] * (DB + 1),
        out_shape=jax.ShapeDtypeStruct((OWNERS * TOK, OWN * FBLK), jnp.bfloat16),
        cost_estimate=cost(1 << 30, 4 << 20),
        compiler_params=params(32),
    )(info, group_ids, *slots)

    rest, dense = lax.optimization_barrier((rest, dense))
    rest_across = lax.ppermute(rest, "core", across)
    side = core.astype(jnp.int32).reshape(1)
    out = product(side, own, rest, dense, None)
    out = product(1 - side, first_across, rest_across, dense, out)
    return out[:, None]


def solution(mesh):
    grid = Mesh(mesh.devices.reshape(DB, FB, 8, 2), ("y", "z", "x", "core"))
    owner, block = ("x", "core"), ("y", "z")
    placed = (P(owner, block, None), P(owner, block, None, None), P(owner, None, None))
    return jax.shard_map(
        body, mesh=grid, in_specs=placed, out_specs=P(owner, block, None, None), check_vma=False
    )
```

```python
import jax
import jax.numpy as jnp
from jax import lax
from jax.experimental import pallas as pl
from jax.experimental.pallas import tpu as pltpu
from jax.sharding import Mesh, PartitionSpec as P

DB = 8
FB = 8
TOP = 8
TOK = 128
DBLK = 896
FBLK = 256
PIECE = FBLK // DB
EXPERTS = 32
CAP = 48
OWN = 2
OWNERS = 16
HALF = CAP // 2
LANES = 128
XS = 8
OWNER = ("x", "core")


def earlier():
    row = lax.broadcasted_iota(jnp.int32, (TOK, TOK), 0)
    col = lax.broadcasted_iota(jnp.int32, (TOK, TOK), 1)
    return (row < col).astype(jnp.bfloat16)


def place_kernel(ids_ref, onehot_ref):
    expert = lax.broadcasted_iota(jnp.int32, (EXPERTS, TOK), 0)
    named = jnp.zeros((EXPERTS, TOK), jnp.float32)
    for k in range(TOP):
        named += (ids_ref[k : k + 1, :] == expert).astype(jnp.float32)
    before = jnp.dot(named.astype(jnp.bfloat16), earlier(), preferred_element_type=jnp.float32)
    place = before.astype(jnp.int32) + CAP * expert
    row = lax.broadcasted_iota(jnp.int32, (OWNERS * HALF, TOK), 0)
    owner = row // HALF
    base = owner * (OWN * CAP) + (row - owner * HALF)
    for k in range(TOP):
        target = jnp.sum(
            jnp.where(ids_ref[k : k + 1, :] == expert, place, 0), axis=0, keepdims=True
        )
        for j in range(4):
            at = (j * TOP + k) * TOK
            onehot_ref[:, at : at + TOK] = (base + j * HALF == target).astype(jnp.bfloat16)


def route_kernel(pieces_ref, onehot_ref, ids_ref, out_ref):
    pieces = pieces_ref[...].astype(jnp.float32)
    block = lax.broadcasted_iota(jnp.int32, (TOK, LANES), 1) // PIECE
    rows = []
    for j in range(4):
        for k in range(TOP):
            half = pieces[:, (k // 4) * LANES : (k // 4 + 1) * LANES]
            shift = ((j - k) % 4) * PIECE
            moved = pltpu.roll(half, shift, 1) if shift else half
            rows.append(jnp.where(block == j, moved, 0.0).astype(jnp.bfloat16))
    routed = jnp.dot(
        onehot_ref[...], jnp.concatenate(rows, axis=0), preferred_element_type=jnp.float32
    )
    ids = ids_ref[...].astype(jnp.float32)
    for d in range(OWNERS):
        out_ref[d] = jnp.concatenate(
            [routed[d * HALF : (d + 1) * HALF], ids], axis=0
        ).astype(jnp.bfloat16)


def copies_kernel(routed_ref, after_ref, slots_ref):
    del after_ref
    for g in range(OWNERS):
        slots = routed_ref[g].astype(jnp.float32)[:HALF].astype(jnp.bfloat16)
        for y in range(DB):
            slots_ref[y, g] = slots


def both_kernel(mine_ref, other_ref, after_ref, out_ref):
    del after_ref
    out_ref[0] = mine_ref[...]
    out_ref[1] = other_ref[...]


def group_order(me):
    x, core = me // 2, me % 2
    step = 1 - 2 * core
    order = []
    for away, first in (
        (0, core),
        (-1, core),
        (1, 1 - core),
        (-2, core),
        (2, 1 - core),
        (-3, core),
        (3, 1 - core),
        (4, core),
    ):
        chip = (x + away * step + XS) % XS
        order += [2 * chip + first, 2 * chip + 1 - first]
    return order


def dense_kernel(me_ref, routed_ref, slots_ref, dense_ref, value_ref):
    source = lax.broadcasted_iota(jnp.int32, (DB * LANES, FBLK), 0)
    column = lax.broadcasted_iota(jnp.int32, (DB * LANES, FBLK), 1)
    lane = source % LANES
    wanted = (source // LANES) * PIECE + lane % PIECE
    slots = jnp.concatenate([slots_ref[y] for y in range(DB)], axis=1)
    spread = []
    for j in range(4):
        pick = ((column == wanted) & (lane // PIECE == j)).astype(jnp.bfloat16)
        spread.append(jnp.dot(slots, pick, preferred_element_type=jnp.float32))
    for e in range(OWN):
        for g in range(OWNERS):
            rows = slice(g * HALF, (g + 1) * HALF)
            value_ref[e, g] = jnp.concatenate(
                [spread[2 * e][rows], spread[2 * e + 1][rows]], axis=0
            ).astype(jnp.bfloat16)
    order = group_order(me_ref[0])
    named = []
    for e in range(OWN):
        for i in range(OWNERS):
            ids = routed_ref[order[i]].astype(jnp.float32)[HALF:].astype(jnp.int32)
            hit = (ids == OWN * me_ref[0] + e).astype(jnp.float32)
            named.append(jnp.sum(hit, axis=0, keepdims=True))
    named = jnp.concatenate(named, axis=0)
    before = jnp.dot(named.astype(jnp.bfloat16), earlier(), preferred_element_type=jnp.float32)
    place = jnp.where(named > 0.0, before, -1.0).T
    number = lax.broadcasted_iota(jnp.int32, (TOK, CAP), 1).astype(jnp.float32)
    for e in range(OWN):
        for i in range(OWNERS):
            at = e * OWNERS + i
            pick = (place[:, at : at + 1] == number).astype(jnp.bfloat16)
            dense_ref[i * TOK : (i + 1) * TOK, e * FBLK : (e + 1) * FBLK] = jnp.dot(
                pick, value_ref[e, order[i]], preferred_element_type=jnp.float32
            ).astype(jnp.bfloat16)


def product_kernel(dense_ref, *refs):
    out_ref = refs[-1]
    left = []
    for ref in refs[:-1]:
        left += [ref[i] for i in range(ref.shape[0])]
    total = jnp.dot(
        jnp.concatenate(left, axis=1), dense_ref[...], preferred_element_type=jnp.float32
    )
    for e in range(OWN):
        out_ref[e] = total[:, e * FBLK : (e + 1) * FBLK].astype(jnp.bfloat16)


def params(mib):
    return pltpu.CompilerParams(vmem_limit_bytes=mib << 20)


def cost(flops, size):
    return pl.CostEstimate(flops=flops, bytes_accessed=size, transcendentals=0)


def ahead(value, steps):
    pairs = []
    for x in range(XS):
        pairs += [(2 * x, 2 * ((x + steps) % XS)), (2 * x + 1, 2 * ((x - steps) % XS) + 1)]
    return lax.ppermute(value, OWNER, pairs)


def swap(value):
    return lax.ppermute(value, "core", [(0, 1), (1, 0)])


def body(tokens, slot_grads, expert_ids):
    ids = expert_ids[0].T
    onehot = pl.pallas_call(
        place_kernel,
        out_shape=jax.ShapeDtypeStruct((OWNERS * HALF, 4 * TOP * TOK), jnp.bfloat16),
        cost_estimate=cost(1 << 22, 6 << 20),
        compiler_params=params(16),
    )(ids)

    x_part = tokens[0].reshape(2, DB, DBLK).transpose(1, 0, 2)
    x_part = jnp.broadcast_to(x_part[:, None], (DB, FB, 2, DBLK))
    g_part = slot_grads[0].reshape(2, TOP, FB, DB, PIECE).transpose(3, 2, 0, 1, 4)
    g_part = g_part.reshape(DB, FB, 2, TOP * PIECE)
    send = jnp.concatenate([x_part, g_part], axis=3).reshape(DB * FB, 2, DBLK + FBLK)
    got = lax.all_to_all(send, ("y", "z"), split_axis=0, concat_axis=0, tiled=True)
    got = got.reshape(TOK, DBLK + FBLK)

    pieces = got[:, DBLK:]
    mine = got[:, :DBLK].T
    mine, pieces = lax.optimization_barrier((mine, pieces))
    other = swap(mine)
    here = pl.pallas_call(
        both_kernel,
        in_specs=[
            pl.BlockSpec(memory_space=pltpu.VMEM),
            pl.BlockSpec(memory_space=pltpu.VMEM),
            pl.BlockSpec(memory_space=pl.ANY),
        ],
        out_shape=jax.ShapeDtypeStruct((2, DBLK, TOK), jnp.bfloat16),
        cost_estimate=cost(1 << 20, 1 << 20),
        compiler_params=params(8),
    )(mine, other, onehot)
    near = ahead(here, 1)
    next_ = ahead(here, 2)
    third = ahead(next_, 1)
    far = ahead(next_, 2)

    routed = pl.pallas_call(
        route_kernel,
        out_shape=jax.ShapeDtypeStruct((OWNERS, HALF + TOP, LANES), jnp.bfloat16),
        cost_estimate=cost(1 << 29, 4 << 20),
        compiler_params=params(16),
    )(pieces, onehot, ids)
    routed, here = lax.optimization_barrier((routed, here))
    routed = lax.all_to_all(routed, OWNER, split_axis=0, concat_axis=0, tiled=True)
    slots = pl.pallas_call(
        copies_kernel,
        in_specs=[
            pl.BlockSpec(memory_space=pltpu.VMEM),
            pl.BlockSpec(memory_space=pl.ANY),
        ],
        out_shape=jax.ShapeDtypeStruct((DB, OWNERS, HALF, LANES), jnp.bfloat16),
        cost_estimate=cost(1 << 20, 1 << 20),
        compiler_params=params(16),
    )(routed, next_)
    slots = lax.all_to_all(slots, "y", split_axis=0, concat_axis=0, tiled=True)

    me = lax.axis_index(OWNER).astype(jnp.int32).reshape(1)
    dense = pl.pallas_call(
        dense_kernel,
        in_specs=[
            pl.BlockSpec(memory_space=pltpu.SMEM),
            pl.BlockSpec(memory_space=pltpu.VMEM),
            pl.BlockSpec(memory_space=pltpu.VMEM),
        ],
        out_shape=jax.ShapeDtypeStruct((OWNERS * TOK, OWN * FBLK), jnp.bfloat16),
        scratch_shapes=[pltpu.VMEM((OWN, OWNERS, CAP, FBLK), jnp.bfloat16)],
        cost_estimate=cost(1 << 30, 4 << 20),
        compiler_params=params(16),
    )(me, routed, slots.reshape(DB, OWNERS * HALF, LANES))

    parts = [here, near, swap(near), next_, swap(next_), third, swap(third), far]
    out = pl.pallas_call(
        product_kernel,
        out_shape=jax.ShapeDtypeStruct((OWN, DBLK, FBLK), jnp.bfloat16),
        cost_estimate=cost(2 * DBLK * 2048 * 512, 7 << 20),
        compiler_params=params(24),
    )(dense, *parts)
    return out[:, None]


def solution(mesh):
    grid = Mesh(mesh.devices.reshape(DB, FB, XS, 2), ("y", "z", "x", "core"))
    owner, block = OWNER, ("y", "z")
    placed = (P(owner, block, None), P(owner, block, None, None), P(owner, None, None))
    return jax.shard_map(
        body, mesh=grid, in_specs=placed, out_specs=P(owner, block, None, None), check_vma=False
    )
```

```python
import jax
import jax.numpy as jnp
from jax import lax
from jax.experimental import pallas as pl
from jax.experimental.pallas import tpu as pltpu
from jax.sharding import Mesh, PartitionSpec as P

DB = 8
FB = 8
TOP = 8
TOK = 128
DBLK = 896
FBLK = 256
PIECE = FBLK // DB
EXPERTS = 32
CAP = 48
OWN = 2
OWNERS = 16
HALF = CAP // 2
LANES = 128
FIRST = 5
PAIRS = 8
ROOM = 64
XS = 8
OWNER = ("x", "core")


def earlier():
    row = lax.broadcasted_iota(jnp.int32, (TOK, TOK), 0)
    col = lax.broadcasted_iota(jnp.int32, (TOK, TOK), 1)
    return (row < col).astype(jnp.bfloat16)


def place_kernel(ids_ref, onehot_ref):
    expert = lax.broadcasted_iota(jnp.int32, (EXPERTS, TOK), 0)
    named = jnp.zeros((EXPERTS, TOK), jnp.float32)
    for k in range(TOP):
        named += (ids_ref[k : k + 1, :] == expert).astype(jnp.float32)
    before = jnp.dot(named.astype(jnp.bfloat16), earlier(), preferred_element_type=jnp.float32)
    place = before.astype(jnp.int32) + CAP * expert
    row = lax.broadcasted_iota(jnp.int32, (OWNERS * HALF, TOK), 0)
    owner = row // HALF
    base = owner * (OWN * CAP) + (row - owner * HALF)
    for k in range(TOP):
        target = jnp.sum(
            jnp.where(ids_ref[k : k + 1, :] == expert, place, 0), axis=0, keepdims=True
        )
        for j in range(4):
            at = (j * TOP + k) * TOK
            onehot_ref[:, at : at + TOK] = (base + j * HALF == target).astype(jnp.bfloat16)


def route_kernel(pieces_ref, onehot_ref, ids_ref, out_ref):
    pieces = pieces_ref[...].astype(jnp.float32)
    block = lax.broadcasted_iota(jnp.int32, (TOK, LANES), 1) // PIECE
    rows = []
    for j in range(4):
        for k in range(TOP):
            half = pieces[:, (k // 4) * LANES : (k // 4 + 1) * LANES]
            shift = ((j - k) % 4) * PIECE
            moved = pltpu.roll(half, shift, 1) if shift else half
            rows.append(jnp.where(block == j, moved, 0.0).astype(jnp.bfloat16))
    routed = jnp.dot(
        onehot_ref[...], jnp.concatenate(rows, axis=0), preferred_element_type=jnp.float32
    )
    ids = ids_ref[...].astype(jnp.float32)
    for d in range(OWNERS):
        out_ref[d] = jnp.concatenate(
            [routed[d * HALF : (d + 1) * HALF], ids], axis=0
        ).astype(jnp.bfloat16)


def copies_kernel(routed_ref, after_ref, slots_ref):
    del after_ref
    for g in range(OWNERS):
        slots = routed_ref[g].astype(jnp.float32)[:HALF].astype(jnp.bfloat16)
        for y in range(DB):
            slots_ref[y, g] = slots


def send_kernel(tokens_ref, grads_ref, out_ref):
    for y in range(DB):
        block = tokens_ref[:, y * DBLK : (y + 1) * DBLK]
        for z in range(FB):
            out_ref[y * FB + z, :, :DBLK] = block
    lane = lax.broadcasted_iota(jnp.int32, (TOP, FBLK), 1)
    row = lax.broadcasted_iota(jnp.int32, (TOP, FBLK), 0)
    turn = (lane // PIECE + DB - row) % DB
    for z in range(FB):
        turned = []
        for i in range(2):
            block = grads_ref[i, :, z * FBLK : (z + 1) * FBLK].astype(jnp.float32)
            value = block
            for by in range(1, DB):
                moved = pltpu.roll(pltpu.roll(block, by * PIECE, 1), DB - by, 0)
                value = jnp.where(turn == by, moved, value)
            turned.append(value)
        for y in range(DB):
            out_ref[y * FB + z, :, DBLK:] = jnp.concatenate(
                [value[y : y + 1] for value in turned], axis=0
            ).astype(jnp.bfloat16)


def both_kernel(mine_ref, other_ref, after_ref, out_ref):
    del after_ref
    out_ref[0] = mine_ref[...]
    out_ref[1] = other_ref[...]


def group_order(me):
    x, core = me // 2, me % 2
    step = 1 - 2 * core
    order = []
    for away, first in (
        (0, core),
        (-1, core),
        (-2, core),
        (2, 1 - core),
        (-3, core),
        (1, 1 - core),
        (3, 1 - core),
        (4, core),
    ):
        chip = (x + away * step + XS) % XS
        order += [2 * chip + first, 2 * chip + 1 - first]
    return order


def pair_rows(ref):
    return jnp.concatenate([ref[0], ref[1]], axis=1)


def early_kernel(me_ref, routed_ref, *refs):
    parts, out_ref = refs[:FIRST], refs[-1]
    order = group_order(me_ref[0])
    named = []
    for i in range(OWNERS):
        ids = routed_ref[order[i]].astype(jnp.float32)[HALF:].astype(jnp.int32)
        for e in range(OWN):
            hit = (ids == OWN * me_ref[0] + e).astype(jnp.float32)
            named.append(jnp.sum(hit, axis=0, keepdims=True))
    named = jnp.concatenate(named, axis=0)
    before = jnp.dot(named.astype(jnp.bfloat16), earlier(), preferred_element_type=jnp.float32)
    place = jnp.where(named > 0.0, before, -1.0).T
    lane = lax.broadcasted_iota(jnp.int32, (TOK, 4 * ROOM), 1)
    number = (lane % ROOM).astype(jnp.float32)
    for p in range(PAIRS):
        halves = []
        for h in range(2):
            at = 2 * (2 * p + h)
            slot = jnp.where(lane < 2 * ROOM, place[:, at : at + 1], place[:, at + 1 : at + 2])
            mine = (slot == number) & ((lane // ROOM) % 2 == h)
            halves.append(mine.astype(jnp.bfloat16))
        pick = jnp.concatenate(halves, axis=0)
        if p < FIRST:
            out_ref[p * DBLK : (p + 1) * DBLK, :] = jnp.dot(
                pair_rows(parts[p]), pick, preferred_element_type=jnp.float32
            ).astype(jnp.bfloat16)
        else:
            at = FIRST * DBLK + (p - FIRST) * 2 * TOK
            out_ref[at : at + 2 * TOK, :] = pick


def value_kernel(slots_ref, value_ref):
    rows = OWNERS * HALF
    halves = []
    for h in range(2):
        halves.append(jnp.concatenate([slots_ref[4 * h + b] for b in range(4)], axis=1))
    row = lax.broadcasted_iota(jnp.int32, (4 * LANES, 4 * LANES), 0)
    col = lax.broadcasted_iota(jnp.int32, (4 * LANES, 4 * LANES), 1)
    same = row % PIECE + (row // LANES) * PIECE == col % LANES
    spread = (same & ((row % LANES) // PIECE == col // LANES)).astype(jnp.bfloat16)
    spread = jnp.dot(
        jnp.concatenate(halves, axis=0), spread, preferred_element_type=jnp.float32
    )
    empty = jnp.zeros((ROOM - CAP, FBLK), jnp.float32)
    for e in range(OWN):
        for g in range(OWNERS):
            value = []
            for j in (2 * e, 2 * e + 1):
                lanes = slice(j * LANES, (j + 1) * LANES)
                left = spread[g * HALF : (g + 1) * HALF, lanes]
                right = spread[rows + g * HALF : rows + (g + 1) * HALF, lanes]
                value.append(jnp.concatenate([left, right], axis=1))
            value_ref[e, g] = jnp.concatenate(value + [empty], axis=0).astype(jnp.bfloat16)


def sums(packed, value_ref, order, e):
    lanes = slice(2 * e * ROOM, 2 * (e + 1) * ROOM)
    left = jnp.concatenate([value[:, lanes] for value in packed], axis=1)
    right = jnp.concatenate([value_ref[e, g] for g in order], axis=0)
    return jnp.dot(left, right, preferred_element_type=jnp.float32)


def first_kernel(me_ref, value_ref, early_ref, total_ref, right_ref):
    order = group_order(me_ref[0])[: 2 * FIRST]
    packed = [early_ref[p * DBLK : (p + 1) * DBLK, :] for p in range(FIRST)]
    for e in range(OWN):
        for i, g in enumerate(order):
            right_ref[e, i * ROOM : (i + 1) * ROOM, :] = value_ref[e, g]
    for e in range(OWN):
        lanes = slice(2 * e * ROOM, 2 * (e + 1) * ROOM)
        left = jnp.concatenate([value[:, lanes] for value in packed], axis=1)
        total_ref[e] = jnp.dot(left, right_ref[e], preferred_element_type=jnp.float32)


def last_kernel(me_ref, value_ref, early_ref, total_ref, *refs):
    out_ref = refs[-1]
    order = group_order(me_ref[0])[2 * FIRST :]
    packed = []
    for p in range(PAIRS - FIRST):
        at = FIRST * DBLK + p * 2 * TOK
        packed.append(
            jnp.dot(
                pair_rows(refs[p]), early_ref[at : at + 2 * TOK, :], preferred_element_type=jnp.float32
            ).astype(jnp.bfloat16)
        )
    for e in range(OWN):
        out_ref[e] = (total_ref[e] + sums(packed, value_ref, order, e)).astype(jnp.bfloat16)


def params(mib):
    return pltpu.CompilerParams(vmem_limit_bytes=mib << 20)


def cost(flops, size):
    return pl.CostEstimate(flops=flops, bytes_accessed=size, transcendentals=0)


def ahead(value, steps):
    pairs = []
    for x in range(XS):
        pairs += [(2 * x, 2 * ((x + steps) % XS)), (2 * x + 1, 2 * ((x - steps) % XS) + 1)]
    return lax.ppermute(value, OWNER, pairs)


def swap(value):
    return lax.ppermute(value, "core", [(0, 1), (1, 0)])


def body(tokens, slot_grads, expert_ids):
    ids = expert_ids[0].T
    onehot = pl.pallas_call(
        place_kernel,
        out_shape=jax.ShapeDtypeStruct((OWNERS * HALF, 4 * TOP * TOK), jnp.bfloat16),
        cost_estimate=cost(1 << 22, 6 << 20),
        compiler_params=params(16),
    )(ids)

    send = pl.pallas_call(
        send_kernel,
        out_shape=jax.ShapeDtypeStruct((DB * FB, 2, DBLK + FBLK), jnp.bfloat16),
        cost_estimate=cost(1 << 31, 1 << 19),
        compiler_params=params(16),
    )(tokens[0], slot_grads[0])
    got = lax.all_to_all(send, ("y", "z"), split_axis=0, concat_axis=0, tiled=True)
    got = got.reshape(TOK, DBLK + FBLK)

    pieces = got[:, DBLK:]
    mine = got[:, :DBLK].T
    mine, pieces = lax.optimization_barrier((mine, pieces))
    other = swap(mine)
    here = pl.pallas_call(
        both_kernel,
        in_specs=[
            pl.BlockSpec(memory_space=pltpu.VMEM),
            pl.BlockSpec(memory_space=pltpu.VMEM),
            pl.BlockSpec(memory_space=pl.ANY),
        ],
        out_shape=jax.ShapeDtypeStruct((2, DBLK, TOK), jnp.bfloat16),
        cost_estimate=cost(1 << 20, 1 << 20),
        compiler_params=params(8),
    )(mine, other, onehot)
    near = ahead(here, 1)
    next_ = ahead(here, 2)
    third = ahead(next_, 1)
    far = ahead(next_, 2)

    routed = pl.pallas_call(
        route_kernel,
        out_shape=jax.ShapeDtypeStruct((OWNERS, HALF + TOP, LANES), jnp.bfloat16),
        cost_estimate=cost(1 << 29, 4 << 20),
        compiler_params=params(16),
    )(pieces, onehot, ids)
    routed, here = lax.optimization_barrier((routed, here))
    routed = lax.all_to_all(routed, OWNER, split_axis=0, concat_axis=0, tiled=True)
    slots = pl.pallas_call(
        copies_kernel,
        in_specs=[
            pl.BlockSpec(memory_space=pltpu.VMEM),
            pl.BlockSpec(memory_space=pl.ANY),
        ],
        out_shape=jax.ShapeDtypeStruct((DB, OWNERS, HALF, LANES), jnp.bfloat16),
        cost_estimate=cost(1 << 20, 1 << 20),
        compiler_params=params(16),
    )(routed, next_)
    slots = lax.all_to_all(slots, "y", split_axis=0, concat_axis=0, tiled=True)

    me = lax.axis_index(OWNER).astype(jnp.int32).reshape(1)
    scalar, vmem = pl.BlockSpec(memory_space=pltpu.SMEM), pl.BlockSpec(memory_space=pltpu.VMEM)
    early = pl.pallas_call(
        early_kernel,
        in_specs=[scalar] + [vmem] * (1 + FIRST),
        out_shape=jax.ShapeDtypeStruct(
            (FIRST * DBLK + (PAIRS - FIRST) * 2 * TOK, 4 * ROOM), jnp.bfloat16
        ),
        cost_estimate=cost(1 << 30, 4 << 20),
        compiler_params=params(60),
    )(me, routed, here, near, next_, swap(next_), third)
    value = pl.pallas_call(
        value_kernel,
        out_shape=jax.ShapeDtypeStruct((OWN, OWNERS, ROOM, FBLK), jnp.bfloat16),
        cost_estimate=cost(1 << 32, 2 << 20),
        compiler_params=params(12),
    )(slots.reshape(DB, OWNERS * HALF, LANES))
    total = pl.pallas_call(
        first_kernel,
        in_specs=[scalar, vmem, vmem],
        out_shape=jax.ShapeDtypeStruct((OWN, DBLK, FBLK), jnp.float32),
        scratch_shapes=[pltpu.VMEM((OWN, 2 * FIRST * ROOM, FBLK), jnp.bfloat16)],
        cost_estimate=cost(1 << 30, 4 << 20),
        compiler_params=params(16),
    )(me, value, early)
    out = pl.pallas_call(
        last_kernel,
        in_specs=[scalar] + [vmem] * (3 + PAIRS - FIRST),
        out_shape=jax.ShapeDtypeStruct((OWN, DBLK, FBLK), jnp.bfloat16),
        cost_estimate=cost(1 << 30, 5 << 20),
        compiler_params=params(16),
    )(me, value, early, total, swap(near), swap(third), far)
    return out[:, None]


def solution(mesh):
    grid = Mesh(mesh.devices.reshape(DB, FB, XS, 2), ("y", "z", "x", "core"))
    owner, block = OWNER, ("y", "z")
    placed = (P(owner, block, None), P(owner, block, None, None), P(owner, None, None))
    return jax.shard_map(
        body, mesh=grid, in_specs=placed, out_specs=P(owner, block, None, None), check_vma=False
    )
```

```python
import jax
import jax.numpy as jnp
from jax import lax
from jax.experimental import pallas as pl
from jax.experimental.pallas import tpu as pltpu
from jax.sharding import Mesh, PartitionSpec as P

DB = 8
FB = 8
TOP = 8
TOK = 128
DBLK = 896
FBLK = 256
PIECE = FBLK // DB
EXPERTS = 32
CAP = 48
OWN = 2
OWNERS = 16
HALF = CAP // 2
LANES = 128
FIRST = 5
PAIRS = 8
ROOM = 64
XS = 8
OWNER = ("x", "core")


def earlier():
    row = lax.broadcasted_iota(jnp.int32, (TOK, TOK), 0)
    col = lax.broadcasted_iota(jnp.int32, (TOK, TOK), 1)
    return (row < col).astype(jnp.bfloat16)


def place_kernel(ids_ref, onehot_ref):
    expert = lax.broadcasted_iota(jnp.int32, (EXPERTS, TOK), 0)
    named = jnp.zeros((EXPERTS, TOK), jnp.float32)
    for k in range(TOP):
        named += (ids_ref[k : k + 1, :] == expert).astype(jnp.float32)
    before = jnp.dot(named.astype(jnp.bfloat16), earlier(), preferred_element_type=jnp.float32)
    place = before.astype(jnp.int32) + CAP * expert
    row = lax.broadcasted_iota(jnp.int32, (OWNERS * HALF, TOK), 0)
    owner = row // HALF
    base = owner * (OWN * CAP) + (row - owner * HALF)
    for k in range(TOP):
        target = jnp.sum(
            jnp.where(ids_ref[k : k + 1, :] == expert, place, 0), axis=0, keepdims=True
        )
        for j in range(4):
            at = (j * TOP + k) * TOK
            onehot_ref[:, at : at + TOK] = (base + j * HALF == target).astype(jnp.bfloat16)


def route_kernel(pieces_ref, onehot_ref, ids_ref, out_ref):
    pieces = pieces_ref[...].astype(jnp.float32)
    block = lax.broadcasted_iota(jnp.int32, (TOK, LANES), 1) // PIECE
    rows = []
    for j in range(4):
        for k in range(TOP):
            half = pieces[:, (k // 4) * LANES : (k // 4 + 1) * LANES]
            shift = ((j - k) % 4) * PIECE
            moved = pltpu.roll(half, shift, 1) if shift else half
            rows.append(jnp.where(block == j, moved, 0.0).astype(jnp.bfloat16))
    routed = jnp.dot(
        onehot_ref[...], jnp.concatenate(rows, axis=0), preferred_element_type=jnp.float32
    )
    ids = ids_ref[...].astype(jnp.float32)
    for d in range(OWNERS):
        out_ref[d] = jnp.concatenate(
            [routed[d * HALF : (d + 1) * HALF], ids], axis=0
        ).astype(jnp.bfloat16)


def copies_kernel(routed_ref, after_ref, slots_ref, block_ref, sems):
    del after_ref
    block_ref[...] = jnp.concatenate(
        [routed_ref[g].astype(jnp.float32)[:HALF] for g in range(OWNERS)], axis=0
    ).astype(jnp.bfloat16)
    copies = [
        pltpu.make_async_copy(block_ref, slots_ref.at[y], sems.at[y]) for y in range(DB)
    ]
    for copy in copies:
        copy.start()
    for copy in copies:
        copy.wait()


def send_kernel(tokens_ref, grads_ref, out_ref):
    for y in range(DB):
        block = tokens_ref[:, y * DBLK : (y + 1) * DBLK]
        for z in range(FB):
            out_ref[y * FB + z, :, :DBLK] = block
    lane = lax.broadcasted_iota(jnp.int32, (TOP, FBLK), 1)
    row = lax.broadcasted_iota(jnp.int32, (TOP, FBLK), 0)
    turn = (lane // PIECE + DB - row) % DB
    for z in range(FB):
        turned = []
        for i in range(2):
            block = grads_ref[i, :, z * FBLK : (z + 1) * FBLK].astype(jnp.float32)
            value = block
            for by in range(1, DB):
                moved = pltpu.roll(pltpu.roll(block, by * PIECE, 1), DB - by, 0)
                value = jnp.where(turn == by, moved, value)
            turned.append(value)
        for y in range(DB):
            out_ref[y * FB + z, :, DBLK:] = jnp.concatenate(
                [value[y : y + 1] for value in turned], axis=0
            ).astype(jnp.bfloat16)


def both_kernel(mine_ref, other_ref, after_ref, out_ref):
    del after_ref
    out_ref[0] = mine_ref[...]
    out_ref[1] = other_ref[...]


def group_order(me):
    x, core = me // 2, me % 2
    step = 1 - 2 * core
    order = []
    for away, first in (
        (0, core),
        (-1, core),
        (-2, core),
        (2, 1 - core),
        (-3, core),
        (1, 1 - core),
        (3, 1 - core),
        (4, core),
    ):
        chip = (x + away * step + XS) % XS
        order += [2 * chip + first, 2 * chip + 1 - first]
    return order


def pair_rows(ref):
    return jnp.concatenate([ref[0], ref[1]], axis=1)


def early_kernel(me_ref, routed_ref, *refs):
    parts, out_ref = refs[:FIRST], refs[-1]
    order = group_order(me_ref[0])
    named = []
    for i in range(OWNERS):
        ids = routed_ref[order[i]].astype(jnp.float32)[HALF:].astype(jnp.int32)
        for e in range(OWN):
            hit = (ids == OWN * me_ref[0] + e).astype(jnp.float32)
            named.append(jnp.sum(hit, axis=0, keepdims=True))
    named = jnp.concatenate(named, axis=0)
    before = jnp.dot(named.astype(jnp.bfloat16), earlier(), preferred_element_type=jnp.float32)
    place = jnp.where(named > 0.0, before, -1.0).T
    lane = lax.broadcasted_iota(jnp.int32, (TOK, 4 * ROOM), 1)
    number = (lane % ROOM).astype(jnp.float32)
    for p in range(PAIRS):
        halves = []
        for h in range(2):
            at = 2 * (2 * p + h)
            slot = jnp.where(lane < 2 * ROOM, place[:, at : at + 1], place[:, at + 1 : at + 2])
            mine = (slot == number) & ((lane // ROOM) % 2 == h)
            halves.append(mine.astype(jnp.bfloat16))
        pick = jnp.concatenate(halves, axis=0)
        if p < FIRST:
            out_ref[p * DBLK : (p + 1) * DBLK, :] = jnp.dot(
                pair_rows(parts[p]), pick, preferred_element_type=jnp.float32
            ).astype(jnp.bfloat16)
        else:
            at = FIRST * DBLK + (p - FIRST) * 2 * TOK
            out_ref[at : at + 2 * TOK, :] = pick


def value_kernel(slots_ref, value_ref):
    rows = OWNERS * HALF
    halves = []
    for h in range(2):
        halves.append(jnp.concatenate([slots_ref[4 * h + b] for b in range(4)], axis=1))
    row = lax.broadcasted_iota(jnp.int32, (4 * LANES, 4 * LANES), 0)
    col = lax.broadcasted_iota(jnp.int32, (4 * LANES, 4 * LANES), 1)
    same = row % PIECE + (row // LANES) * PIECE == col % LANES
    spread = (same & ((row % LANES) // PIECE == col // LANES)).astype(jnp.bfloat16)
    spread = jnp.dot(
        jnp.concatenate(halves, axis=0), spread, preferred_element_type=jnp.float32
    )
    empty = jnp.zeros((ROOM - CAP, FBLK), jnp.float32)
    for e in range(OWN):
        for g in range(OWNERS):
            value = []
            for j in (2 * e, 2 * e + 1):
                lanes = slice(j * LANES, (j + 1) * LANES)
                left = spread[g * HALF : (g + 1) * HALF, lanes]
                right = spread[rows + g * HALF : rows + (g + 1) * HALF, lanes]
                value.append(jnp.concatenate([left, right], axis=1))
            value_ref[e, g] = jnp.concatenate(value + [empty], axis=0).astype(jnp.bfloat16)


def sums(packed, value_ref, order, e):
    lanes = slice(2 * e * ROOM, 2 * (e + 1) * ROOM)
    left = jnp.concatenate([value[:, lanes] for value in packed], axis=1)
    right = jnp.concatenate([value_ref[e, g] for g in order], axis=0)
    return jnp.dot(left, right, preferred_element_type=jnp.float32)


def first_kernel(me_ref, value_ref, early_ref, total_ref, right_ref):
    order = group_order(me_ref[0])[: 2 * FIRST]
    packed = [early_ref[p * DBLK : (p + 1) * DBLK, :] for p in range(FIRST)]
    for e in range(OWN):
        for i, g in enumerate(order):
            right_ref[e, i * ROOM : (i + 1) * ROOM, :] = value_ref[e, g]
    for e in range(OWN):
        lanes = slice(2 * e * ROOM, 2 * (e + 1) * ROOM)
        left = jnp.concatenate([value[:, lanes] for value in packed], axis=1)
        total_ref[e] = jnp.dot(left, right_ref[e], preferred_element_type=jnp.float32)


def last_kernel(me_ref, value_ref, early_ref, total_ref, *refs):
    out_ref = refs[-1]
    order = group_order(me_ref[0])[2 * FIRST :]
    packed = []
    for p in range(PAIRS - FIRST):
        at = FIRST * DBLK + p * 2 * TOK
        packed.append(
            jnp.dot(
                pair_rows(refs[p]), early_ref[at : at + 2 * TOK, :], preferred_element_type=jnp.float32
            ).astype(jnp.bfloat16)
        )
    for e in range(OWN):
        out_ref[e] = (total_ref[e] + sums(packed, value_ref, order, e)).astype(jnp.bfloat16)


def params(mib):
    return pltpu.CompilerParams(vmem_limit_bytes=mib << 20)


def cost(flops, size):
    return pl.CostEstimate(flops=flops, bytes_accessed=size, transcendentals=0)


def ahead(value, steps):
    pairs = []
    for x in range(XS):
        pairs += [(2 * x, 2 * ((x + steps) % XS)), (2 * x + 1, 2 * ((x - steps) % XS) + 1)]
    return lax.ppermute(value, OWNER, pairs)


def swap(value):
    return lax.ppermute(value, "core", [(0, 1), (1, 0)])


def body(tokens, slot_grads, expert_ids):
    ids = expert_ids[0].T
    onehot = pl.pallas_call(
        place_kernel,
        out_shape=jax.ShapeDtypeStruct((OWNERS * HALF, 4 * TOP * TOK), jnp.bfloat16),
        cost_estimate=cost(1 << 22, 6 << 20),
        compiler_params=params(16),
    )(ids)

    send = pl.pallas_call(
        send_kernel,
        out_shape=jax.ShapeDtypeStruct((DB * FB, 2, DBLK + FBLK), jnp.bfloat16),
        cost_estimate=cost(1 << 31, 1 << 19),
        compiler_params=params(16),
    )(tokens[0], slot_grads[0])
    got = lax.all_to_all(send, ("y", "z"), split_axis=0, concat_axis=0, tiled=True)
    got = got.reshape(TOK, DBLK + FBLK)

    pieces = got[:, DBLK:]
    mine = got[:, :DBLK].T
    mine, pieces = lax.optimization_barrier((mine, pieces))
    other = swap(mine)
    here = pl.pallas_call(
        both_kernel,
        in_specs=[
            pl.BlockSpec(memory_space=pltpu.VMEM),
            pl.BlockSpec(memory_space=pltpu.VMEM),
            pl.BlockSpec(memory_space=pl.ANY),
        ],
        out_shape=jax.ShapeDtypeStruct((2, DBLK, TOK), jnp.bfloat16),
        cost_estimate=cost(1 << 20, 1 << 20),
        compiler_params=params(8),
    )(mine, other, onehot)
    near = ahead(here, 1)
    next_ = ahead(here, 2)
    third = ahead(next_, 1)
    far = ahead(next_, 2)

    routed = pl.pallas_call(
        route_kernel,
        out_shape=jax.ShapeDtypeStruct((OWNERS, HALF + TOP, LANES), jnp.bfloat16),
        cost_estimate=cost(1 << 29, 4 << 20),
        compiler_params=params(16),
    )(pieces, onehot, ids)
    routed, here = lax.optimization_barrier((routed, here))
    routed = lax.all_to_all(routed, OWNER, split_axis=0, concat_axis=0, tiled=True)
    slots = pl.pallas_call(
        copies_kernel,
        in_specs=[
            pl.BlockSpec(memory_space=pltpu.VMEM),
            pl.BlockSpec(memory_space=pl.ANY),
        ],
        out_specs=pl.BlockSpec(memory_space=pl.ANY),
        out_shape=jax.ShapeDtypeStruct((DB, OWNERS * HALF, LANES), jnp.bfloat16),
        scratch_shapes=[
            pltpu.VMEM((OWNERS * HALF, LANES), jnp.bfloat16),
            pltpu.SemaphoreType.DMA((DB,)),
        ],
        cost_estimate=cost(1 << 20, 1 << 20),
        compiler_params=params(16),
    )(routed, next_)
    slots = lax.all_to_all(slots, "y", split_axis=0, concat_axis=0, tiled=True)

    me = lax.axis_index(OWNER).astype(jnp.int32).reshape(1)
    scalar, vmem = pl.BlockSpec(memory_space=pltpu.SMEM), pl.BlockSpec(memory_space=pltpu.VMEM)
    early = pl.pallas_call(
        early_kernel,
        in_specs=[scalar] + [vmem] * (1 + FIRST),
        out_shape=jax.ShapeDtypeStruct(
            (FIRST * DBLK + (PAIRS - FIRST) * 2 * TOK, 4 * ROOM), jnp.bfloat16
        ),
        cost_estimate=cost(1 << 30, 4 << 20),
        compiler_params=params(60),
    )(me, routed, here, near, next_, swap(next_), third)
    value = pl.pallas_call(
        value_kernel,
        out_shape=jax.ShapeDtypeStruct((OWN, OWNERS, ROOM, FBLK), jnp.bfloat16),
        cost_estimate=cost(1 << 32, 2 << 20),
        compiler_params=params(12),
    )(slots)
    total = pl.pallas_call(
        first_kernel,
        in_specs=[scalar, vmem, vmem],
        out_shape=jax.ShapeDtypeStruct((OWN, DBLK, FBLK), jnp.float32),
        scratch_shapes=[pltpu.VMEM((OWN, 2 * FIRST * ROOM, FBLK), jnp.bfloat16)],
        cost_estimate=cost(1 << 30, 4 << 20),
        compiler_params=params(16),
    )(me, value, early)
    out = pl.pallas_call(
        last_kernel,
        in_specs=[scalar] + [vmem] * (3 + PAIRS - FIRST),
        out_shape=jax.ShapeDtypeStruct((OWN, DBLK, FBLK), jnp.bfloat16),
        cost_estimate=cost(1 << 30, 5 << 20),
        compiler_params=params(16),
    )(me, value, early, total, swap(near), swap(third), far)
    return out[:, None]


def solution(mesh):
    grid = Mesh(mesh.devices.reshape(DB, FB, XS, 2), ("y", "z", "x", "core"))
    owner, block = OWNER, ("y", "z")
    placed = (P(owner, block, None), P(owner, block, None, None), P(owner, None, None))
    return jax.shard_map(
        body, mesh=grid, in_specs=placed, out_specs=P(owner, block, None, None), check_vma=False
    )
```

```python
import jax
import jax.numpy as jnp
from jax import lax
from jax.experimental import pallas as pl
from jax.experimental.pallas import tpu as pltpu
from jax.sharding import Mesh, PartitionSpec as P

DB = 8
FB = 8
TOP = 8
TOK = 128
DBLK = 896
FBLK = 256
PIECE = FBLK // DB
EXPERTS = 32
CAP = 48
OWN = 2
OWNERS = 16
HALF = CAP // 2
LANES = 128
FIRST = 4
PAIRS = 8
ROOM = 64
XS = 8
OWNER = ("x", "core")


def earlier():
    row = lax.broadcasted_iota(jnp.int32, (TOK, TOK), 0)
    col = lax.broadcasted_iota(jnp.int32, (TOK, TOK), 1)
    return (row < col).astype(jnp.bfloat16)


def place_kernel(ids_ref, onehot_ref):
    expert = lax.broadcasted_iota(jnp.int32, (EXPERTS, TOK), 0)
    named = jnp.zeros((EXPERTS, TOK), jnp.float32)
    for k in range(TOP):
        named += (ids_ref[k : k + 1, :] == expert).astype(jnp.float32)
    before = jnp.dot(named.astype(jnp.bfloat16), earlier(), preferred_element_type=jnp.float32)
    place = before.astype(jnp.int32) + CAP * expert
    row = lax.broadcasted_iota(jnp.int32, (OWNERS * HALF, TOK), 0)
    owner = row // HALF
    base = owner * (OWN * CAP) + (row - owner * HALF)
    for k in range(TOP):
        target = jnp.sum(
            jnp.where(ids_ref[k : k + 1, :] == expert, place, 0), axis=0, keepdims=True
        )
        for j in range(4):
            at = (j * TOP + k) * TOK
            onehot_ref[:, at : at + TOK] = (base + j * HALF == target).astype(jnp.bfloat16)


def route_kernel(pieces_ref, onehot_ref, ids_ref, out_ref):
    pieces = pieces_ref[...].astype(jnp.float32)
    block = lax.broadcasted_iota(jnp.int32, (TOK, LANES), 1) // PIECE
    rows = []
    for j in range(4):
        for k in range(TOP):
            half = pieces[:, (k // 4) * LANES : (k // 4 + 1) * LANES]
            shift = ((j - k) % 4) * PIECE
            moved = pltpu.roll(half, shift, 1) if shift else half
            rows.append(jnp.where(block == j, moved, 0.0).astype(jnp.bfloat16))
    routed = jnp.dot(
        onehot_ref[...], jnp.concatenate(rows, axis=0), preferred_element_type=jnp.float32
    )
    ids = ids_ref[...].astype(jnp.float32)
    for d in range(OWNERS):
        out_ref[d] = jnp.concatenate(
            [routed[d * HALF : (d + 1) * HALF], ids], axis=0
        ).astype(jnp.bfloat16)


def copies_kernel(routed_ref, after_ref, slots_ref):
    del after_ref
    for g in range(OWNERS):
        slots = routed_ref[g].astype(jnp.float32)[:HALF].astype(jnp.bfloat16)
        for y in range(DB):
            slots_ref[y, g] = slots


def send_kernel(tokens_ref, grads_ref, out_ref):
    for y in range(DB):
        block = tokens_ref[:, y * DBLK : (y + 1) * DBLK]
        for z in range(FB):
            out_ref[y * FB + z, :, :DBLK] = block
    lane = lax.broadcasted_iota(jnp.int32, (TOP, FBLK), 1)
    row = lax.broadcasted_iota(jnp.int32, (TOP, FBLK), 0)
    turn = (lane // PIECE + DB - row) % DB
    for z in range(FB):
        turned = []
        for i in range(2):
            block = grads_ref[i, :, z * FBLK : (z + 1) * FBLK].astype(jnp.float32)
            value = block
            for by in range(1, DB):
                moved = pltpu.roll(pltpu.roll(block, by * PIECE, 1), DB - by, 0)
                value = jnp.where(turn == by, moved, value)
            turned.append(value)
        for y in range(DB):
            out_ref[y * FB + z, :, DBLK:] = jnp.concatenate(
                [value[y : y + 1] for value in turned], axis=0
            ).astype(jnp.bfloat16)


def both_kernel(mine_ref, other_ref, after_ref, out_ref):
    del after_ref
    out_ref[0] = mine_ref[...]
    out_ref[1] = other_ref[...]


def group_order(me):
    x, core = me // 2, me % 2
    step = 1 - 2 * core
    order = []
    for away, first in (
        (0, core),
        (-1, core),
        (-2, core),
        (-3, core),
        (2, 1 - core),
        (1, 1 - core),
        (3, 1 - core),
        (4, core),
    ):
        chip = (x + away * step + XS) % XS
        order += [2 * chip + first, 2 * chip + 1 - first]
    return order


def pair_rows(ref):
    return jnp.concatenate([ref[0], ref[1]], axis=1)


def early_kernel(me_ref, routed_ref, *refs):
    parts, out_ref = refs[:FIRST], refs[-1]
    order = group_order(me_ref[0])
    named = []
    for i in range(OWNERS):
        ids = routed_ref[order[i]].astype(jnp.float32)[HALF:].astype(jnp.int32)
        for e in range(OWN):
            hit = (ids == OWN * me_ref[0] + e).astype(jnp.float32)
            named.append(jnp.sum(hit, axis=0, keepdims=True))
    named = jnp.concatenate(named, axis=0)
    before = jnp.dot(named.astype(jnp.bfloat16), earlier(), preferred_element_type=jnp.float32)
    place = jnp.where(named > 0.0, before, -1.0).T
    lane = lax.broadcasted_iota(jnp.int32, (TOK, 4 * ROOM), 1)
    number = (lane % ROOM).astype(jnp.float32)
    for p in range(PAIRS):
        halves = []
        for h in range(2):
            at = 2 * (2 * p + h)
            slot = jnp.where(lane < 2 * ROOM, place[:, at : at + 1], place[:, at + 1 : at + 2])
            mine = (slot == number) & ((lane // ROOM) % 2 == h)
            halves.append(mine.astype(jnp.bfloat16))
        pick = jnp.concatenate(halves, axis=0)
        if p < FIRST:
            out_ref[p * DBLK : (p + 1) * DBLK, :] = jnp.dot(
                pair_rows(parts[p]), pick, preferred_element_type=jnp.float32
            ).astype(jnp.bfloat16)
        else:
            at = FIRST * DBLK + (p - FIRST) * 2 * TOK
            out_ref[at : at + 2 * TOK, :] = pick


def value_kernel(slots_ref, value_ref):
    rows = OWNERS * HALF
    halves = []
    for h in range(2):
        halves.append(jnp.concatenate([slots_ref[4 * h + b] for b in range(4)], axis=1))
    row = lax.broadcasted_iota(jnp.int32, (4 * LANES, 4 * LANES), 0)
    col = lax.broadcasted_iota(jnp.int32, (4 * LANES, 4 * LANES), 1)
    same = row % PIECE + (row // LANES) * PIECE == col % LANES
    spread = (same & ((row % LANES) // PIECE == col // LANES)).astype(jnp.bfloat16)
    spread = jnp.dot(
        jnp.concatenate(halves, axis=0), spread, preferred_element_type=jnp.float32
    )
    empty = jnp.zeros((ROOM - CAP, FBLK), jnp.float32)
    for e in range(OWN):
        for g in range(OWNERS):
            value = []
            for j in (2 * e, 2 * e + 1):
                lanes = slice(j * LANES, (j + 1) * LANES)
                left = spread[g * HALF : (g + 1) * HALF, lanes]
                right = spread[rows + g * HALF : rows + (g + 1) * HALF, lanes]
                value.append(jnp.concatenate([left, right], axis=1))
            value_ref[e, g] = jnp.concatenate(value + [empty], axis=0).astype(jnp.bfloat16)


def sums(packed, value_ref, order, e):
    lanes = slice(2 * e * ROOM, 2 * (e + 1) * ROOM)
    left = jnp.concatenate([value[:, lanes] for value in packed], axis=1)
    right = jnp.concatenate([value_ref[e, g] for g in order], axis=0)
    return jnp.dot(left, right, preferred_element_type=jnp.float32)


def first_kernel(me_ref, value_ref, early_ref, total_ref, right_ref):
    order = group_order(me_ref[0])[: 2 * FIRST]
    packed = [early_ref[p * DBLK : (p + 1) * DBLK, :] for p in range(FIRST)]
    for e in range(OWN):
        for i, g in enumerate(order):
            right_ref[e, i * ROOM : (i + 1) * ROOM, :] = value_ref[e, g]
    for e in range(OWN):
        lanes = slice(2 * e * ROOM, 2 * (e + 1) * ROOM)
        left = jnp.concatenate([value[:, lanes] for value in packed], axis=1)
        total_ref[e] = jnp.dot(left, right_ref[e], preferred_element_type=jnp.float32)


def last_kernel(me_ref, value_ref, early_ref, total_ref, *refs):
    out_ref = refs[-1]
    order = group_order(me_ref[0])[2 * FIRST :]
    packed = []
    for p in range(PAIRS - FIRST):
        at = FIRST * DBLK + p * 2 * TOK
        packed.append(
            jnp.dot(
                pair_rows(refs[p]), early_ref[at : at + 2 * TOK, :], preferred_element_type=jnp.float32
            ).astype(jnp.bfloat16)
        )
    for e in range(OWN):
        out_ref[e] = (total_ref[e] + sums(packed, value_ref, order, e)).astype(jnp.bfloat16)


def params(mib):
    return pltpu.CompilerParams(vmem_limit_bytes=mib << 20)


def cost(flops, size):
    return pl.CostEstimate(flops=flops, bytes_accessed=size, transcendentals=0)


def ahead(value, steps):
    pairs = []
    for x in range(XS):
        pairs += [(2 * x, 2 * ((x + steps) % XS)), (2 * x + 1, 2 * ((x - steps) % XS) + 1)]
    return lax.ppermute(value, OWNER, pairs)


def swap(value):
    return lax.ppermute(value, "core", [(0, 1), (1, 0)])


def body(tokens, slot_grads, expert_ids):
    ids = expert_ids[0].T
    onehot = pl.pallas_call(
        place_kernel,
        out_shape=jax.ShapeDtypeStruct((OWNERS * HALF, 4 * TOP * TOK), jnp.bfloat16),
        cost_estimate=cost(1 << 22, 6 << 20),
        compiler_params=params(16),
    )(ids)

    send = pl.pallas_call(
        send_kernel,
        out_shape=jax.ShapeDtypeStruct((DB * FB, 2, DBLK + FBLK), jnp.bfloat16),
        cost_estimate=cost(1 << 31, 1 << 19),
        compiler_params=params(16),
    )(tokens[0], slot_grads[0])
    got = lax.all_to_all(send, ("y", "z"), split_axis=0, concat_axis=0, tiled=True)
    got = got.reshape(TOK, DBLK + FBLK)

    pieces = got[:, DBLK:]
    mine = got[:, :DBLK].T
    mine, pieces = lax.optimization_barrier((mine, pieces))
    other = swap(mine)
    here = pl.pallas_call(
        both_kernel,
        in_specs=[
            pl.BlockSpec(memory_space=pltpu.VMEM),
            pl.BlockSpec(memory_space=pltpu.VMEM),
            pl.BlockSpec(memory_space=pl.ANY),
        ],
        out_shape=jax.ShapeDtypeStruct((2, DBLK, TOK), jnp.bfloat16),
        cost_estimate=cost(1 << 20, 1 << 20),
        compiler_params=params(8),
    )(mine, other, onehot)
    near = ahead(here, 1)
    next_ = ahead(here, 2)
    third = ahead(next_, 1)
    far = ahead(next_, 2)

    routed = pl.pallas_call(
        route_kernel,
        out_shape=jax.ShapeDtypeStruct((OWNERS, HALF + TOP, LANES), jnp.bfloat16),
        cost_estimate=cost(1 << 29, 4 << 20),
        compiler_params=params(16),
    )(pieces, onehot, ids)
    routed, here = lax.optimization_barrier((routed, here))
    routed = lax.all_to_all(routed, OWNER, split_axis=0, concat_axis=0, tiled=True)
    slots = pl.pallas_call(
        copies_kernel,
        in_specs=[
            pl.BlockSpec(memory_space=pltpu.VMEM),
            pl.BlockSpec(memory_space=pl.ANY),
        ],
        out_shape=jax.ShapeDtypeStruct((DB, OWNERS, HALF, LANES), jnp.bfloat16),
        cost_estimate=cost(1 << 20, 1 << 20),
        compiler_params=params(16),
    )(routed, next_)
    slots = lax.all_to_all(slots, "y", split_axis=0, concat_axis=0, tiled=True)

    me = lax.axis_index(OWNER).astype(jnp.int32).reshape(1)
    scalar, vmem = pl.BlockSpec(memory_space=pltpu.SMEM), pl.BlockSpec(memory_space=pltpu.VMEM)
    early = pl.pallas_call(
        early_kernel,
        in_specs=[scalar] + [vmem] * (1 + FIRST),
        out_shape=jax.ShapeDtypeStruct(
            (FIRST * DBLK + (PAIRS - FIRST) * 2 * TOK, 4 * ROOM), jnp.bfloat16
        ),
        cost_estimate=cost(1 << 30, 4 << 20),
        compiler_params=params(60),
    )(me, routed, here, near, next_, third)
    value = pl.pallas_call(
        value_kernel,
        out_shape=jax.ShapeDtypeStruct((OWN, OWNERS, ROOM, FBLK), jnp.bfloat16),
        cost_estimate=cost(1 << 32, 2 << 20),
        compiler_params=params(12),
    )(slots.reshape(DB, OWNERS * HALF, LANES))
    total = pl.pallas_call(
        first_kernel,
        in_specs=[scalar, vmem, vmem],
        out_shape=jax.ShapeDtypeStruct((OWN, DBLK, FBLK), jnp.float32),
        scratch_shapes=[pltpu.VMEM((OWN, 2 * FIRST * ROOM, FBLK), jnp.bfloat16)],
        cost_estimate=cost(1 << 30, 4 << 20),
        compiler_params=params(16),
    )(me, value, early)
    out = pl.pallas_call(
        last_kernel,
        in_specs=[scalar] + [vmem] * (3 + PAIRS - FIRST),
        out_shape=jax.ShapeDtypeStruct((OWN, DBLK, FBLK), jnp.bfloat16),
        cost_estimate=cost(1 << 30, 5 << 20),
        compiler_params=params(16),
    )(me, value, early, total, swap(next_), swap(near), swap(third), far)
    return out[:, None]


def solution(mesh):
    grid = Mesh(mesh.devices.reshape(DB, FB, XS, 2), ("y", "z", "x", "core"))
    owner, block = OWNER, ("y", "z")
    placed = (P(owner, block, None), P(owner, block, None, None), P(owner, None, None))
    return jax.shard_map(
        body, mesh=grid, in_specs=placed, out_specs=P(owner, block, None, None), check_vma=False
    )
```
